32 devices in a mesh: grp: 2 (over x), gx: 16 (over z, y, core).
Axes of the slice: x: 2, y: 2, z: 4, core: 2. Of those that a mesh axis runs over, the one named last changes fastest.
Arguments:
- hidden_in: bfloat16 [8, 16384], P('grp', 'gx'), parts along dimension 0, may hold values from -128 to 128
- norm_gain: bfloat16 [16384], P('gx'), may hold values from 0.099609375 to 1.8984375
- qkv_weight: bfloat16 [16384, 4, 2304], P('gx'), may hold values from -0.046875 to 0.046875
- out_weight: bfloat16 [8192, 16384], P(None, 'gx'), may hold values from -0.0625 to 0.0625
- key_cache: bfloat16 [32, 8192, 128], P(('grp', 'gx')), parts along dimension 0, may hold values from -400 to 400
- value_cache: bfloat16 [32, 8192, 128], P(('grp', 'gx')), parts along dimension 0, may hold values from -6 to 6
- lengths: int32 [8], P('grp'), parts along dimension 0, may hold values from 1024 to 8192, as said below
- positions: int32 [8], P('grp'), parts along dimension 0, may hold values from 0 to 8191
Outputs:
- attention_out: bfloat16 [8, 16384], P('grp', 'gx'), parts along dimension 0
- new_entry: bfloat16 [32, 256], P(('grp', 'gx')), parts along dimension 0
The draws below stay inside these ranges and needn't reach their ends.
There are 2 independent parts, one for each index of `grp`. The reference program is written for one: setup_inputs(seed, part) draws one part's arguments, and reference() takes and returns one part's arrays. A program takes and returns all parts, laid end to end along the dimension named above; an argument that names none is the same for every part. Nothing has to cross between parts.
Inputs may be any that keep to these rules, and one draw needn't show every extreme that they name: `lengths`: some row reaches 8192.
All inputs are finite; a program needn't handle non-finite values.
Results may differ from the reference program's by a relative error of at most 0.012.
Values may be sent and summed in bfloat16 or wider, within the bound.
A program may use at most 128 MiB of HBM per device.

```python
import math
import jax
import jax.numpy as jnp
from jax import lax

D = 16384
HD = 128
HQ = 64
KVH = 4
CTX = 8192
GQA = 16
ROWS = 4


def draw_hidden_in(key, part):
    key = jax.random.fold_in(key, 11)
    key_rows, key_base, key_rough = jax.random.split(key, 3)
    column = jnp.arange(D, dtype=jnp.float32) / D
    roughness = jax.random.uniform(key_rough, (1, D), minval=0.5, maxval=1.5)
    row_scale = jnp.exp(jax.random.uniform(key_rows, (ROWS, 1)) * math.log(10.0))
    column_ramp = jnp.exp(column * 0.5 * math.log(3.0))[None, :]
    values = jnp.clip(jax.random.normal(key_base, (ROWS, D)), -4.0, 4.0)
    return (values * row_scale * column_ramp * roughness).astype(jnp.bfloat16)


def draw_key_cache(key, part):
    key = jax.random.fold_in(key, 23)
    key_base = jax.random.fold_in(key, 0)
    slot_count = KVH * ROWS
    values = jnp.clip(jax.random.normal(key_base, (slot_count, CTX, HD)), -4.0, 4.0) * 2.5
    return values.astype(jnp.bfloat16)


def draw_lengths(key, part):
    key = jax.random.fold_in(key, 37)
    key_len, key_full = jax.random.split(key, 2)
    values = jax.random.randint(key_len, (ROWS,), CTX // 8, CTX + 1)
    full_row = jax.random.randint(key_full, (), 0, ROWS)
    return jnp.where(jnp.arange(ROWS) == full_row, CTX, values).astype(jnp.int32)


def with_ends(values, rng, least, high):
    shape = values.shape
    spot = [jax.random.randint(jax.random.fold_in(rng, axis), (), 0, shape[axis]) for axis in range(len(shape))]
    values = values.at[tuple(spot)].set(least)
    longest = shape.index(max(shape))
    spot[longest] = (spot[longest] + 1) % shape[longest]
    return values.at[tuple(spot)].set(high)


def levels(rng, extent, pieces, least, top_value):
    def one(position, blocks):
        heights = jax.random.uniform(jax.random.fold_in(jax.random.fold_in(rng, 6), position), (blocks,), jnp.float32, least / len(pieces), top_value / len(pieces))
        return jnp.repeat(jnp.exp(heights), extent[position] // blocks).reshape((-1,) + (1,) * (len(extent) - position - 1))

    gain = one(*pieces[0])
    for cut in pieces[1:]:
        gain = gain * one(*cut)
    return gain


def normal_values(rng, shape, deviation, most, cuts=(), kind=jnp.bfloat16):
    result = jax.random.normal(rng, shape, jnp.float32) * deviation
    if len(cuts) > 0:
        result = levels(rng, shape, cuts, -0.22, 0.18) * result
    return jnp.clip(result, min=-most, max=most).astype(kind)


def setup_inputs(seed: int = 0, part: int = 0) -> dict:
    keys = jax.random.split(jax.random.key(seed), 9)
    part_splits = jax.random.split(jax.random.fold_in(keys[8], part), 9)
    hidden_in = draw_hidden_in(jax.random.fold_in(jax.random.fold_in(keys[8], part), 71), part)
    norm_gain = jnp.clip(1.0 + 0.18 * jax.random.normal(keys[1], (D,), jnp.float32), 0.099609375, 1.8984375).astype(jnp.bfloat16)
    qkv_weight = normal_values(keys[2], (D, KVH, (GQA + 2) * HD), D ** -0.5, 0.046875, ((0, 16),))
    out_weight = normal_values(keys[3], (HQ * HD, D), (HQ * HD) ** -0.5, 0.0625, ((1, 16),))
    key_cache = draw_key_cache(jax.random.fold_in(jax.random.fold_in(keys[8], part), 71), part)
    value_cache = normal_values(part_splits[5], (KVH * ROWS, CTX, HD), 1.0, 6.0, ((0, 16),))
    lengths = draw_lengths(jax.random.fold_in(jax.random.fold_in(keys[8], part), 71), part)
    positions = with_ends(jax.random.randint(part_splits[7], (ROWS,), 0, CTX), jax.random.fold_in(part_splits[7], 1), 0, CTX - 1).astype(jnp.int32)
    return {"hidden_in": hidden_in, "norm_gain": norm_gain, "qkv_weight": qkv_weight, "out_weight": out_weight, "key_cache": key_cache, "value_cache": value_cache, "lengths": lengths, "positions": positions}


rope_base = 500000.0
norm_eps = 1e-05

def rotate(vectors, places):
    half_width = vectors.shape[-1] // 2
    frequency = rope_base ** (-(jnp.arange(half_width, dtype=jnp.float32) * 2.0 / vectors.shape[-1]))
    angles = places.astype(jnp.float32)[:, None] * frequency[None, :]
    cosine = jnp.cos(angles)[:, None, :]
    sine_part = jnp.sin(angles)[:, None, :]
    front_half = vectors[..., :half_width]
    second = vectors[..., half_width:]
    return jnp.concatenate([front_half * cosine - second * sine_part, second * cosine + front_half * sine_part], axis=-1)

def attend(packed):
    queries, cached_keys, cached_values, own_key, own_value, length = packed
    score_scale = queries.shape[-1] ** (-0.5)
    scores = jnp.dot(queries, cached_keys.T, preferred_element_type=jnp.float32) * score_scale
    in_range = jnp.arange(cached_keys.shape[0], dtype=jnp.int32) < length
    scores = jnp.where(in_range[None, :], scores, -jnp.inf)
    own_score = jnp.dot(queries, own_key, preferred_element_type=jnp.float32) * score_scale
    highest = jnp.maximum(lax.optimization_barrier(jnp.max(scores, axis=1)), own_score)
    exponent = jnp.exp(scores - highest[:, None])
    own_exponent = jnp.exp(own_score - highest)
    denominator = lax.optimization_barrier(jnp.sum(exponent, axis=1)) + own_exponent
    weights = (exponent / denominator[:, None]).astype(jnp.bfloat16)
    own_weight = (own_exponent / denominator).astype(jnp.bfloat16)
    combined = jnp.dot(weights, cached_values, preferred_element_type=jnp.float32)
    combined = combined + own_weight.astype(jnp.float32)[:, None] * own_value.astype(jnp.float32)[None, :]
    return combined.reshape(-1).astype(jnp.bfloat16)

def reference(hidden_in, norm_gain, qkv_weight, out_weight, key_cache, value_cache, lengths, positions):
    features = hidden_in.astype(jnp.float32)
    inverse = lax.rsqrt(lax.optimization_barrier(jnp.mean(features * features, axis=1, keepdims=True)) + norm_eps)
    normed = (features * inverse * norm_gain.astype(jnp.float32)[None, :]).astype(jnp.bfloat16)
    columns = qkv_weight.shape[2]
    flat_proj = jnp.dot(normed, qkv_weight.reshape(D, KVH * columns), preferred_element_type=jnp.float32)
    projected = flat_proj.reshape(ROWS, KVH, columns).transpose(1, 0, 2).reshape(KVH * ROWS, columns)
    group_width = GQA * HD
    slot_rows = jnp.tile(jnp.arange(ROWS, dtype=jnp.int32), KVH)
    places = positions[slot_rows]
    limits = lengths[slot_rows]
    queries = rotate(projected[:, :group_width].reshape(KVH * ROWS, GQA, HD), places).astype(jnp.bfloat16)
    new_keys = rotate(projected[:, group_width:group_width + HD][:, None, :], places)[:, 0, :].astype(jnp.bfloat16)
    new_values = projected[:, group_width + HD:].astype(jnp.bfloat16)
    new_entry = jnp.concatenate([new_keys, new_values], axis=1)
    heads_out = lax.map(attend, (queries, key_cache, value_cache, new_keys, new_values, limits))
    merged = heads_out.reshape(KVH, ROWS, group_width).transpose(1, 0, 2).reshape(ROWS, KVH * group_width)
    attention_out = jnp.dot(merged, out_weight, preferred_element_type=jnp.float32).astype(jnp.bfloat16)
    return (attention_out, new_entry)
```

```python
import functools

import jax
import jax.numpy as jnp
import numpy as np
from jax import lax
from jax.experimental import pallas as pl
from jax.experimental.pallas import tpu as pltpu
from jax.sharding import PartitionSpec as P

rope_base = 500000.0
norm_eps = 1e-05
MESH = pl.DeviceIdType.MESH
KEY_CHUNKS = 4
WEIGHT_CHUNKS = 16
MSG_ROWS = 32


def attention_kernel(
    n, kv_heads, row_count, features_total,
    lengths_ref, positions_ref, freq_ref, hidden_ref, gain_ref, p_hbm, k_hbm, v_hbm, w_hbm,
    out_ref, entry_ref,
    p_vmem, lhs_ref, part_ref, k_vmem, v_vmem, w_vmem, wide, send_buf, recv_buf, heads_own, heads_all, score_buf, lhs_buf,
    p_sem, k_sem, v_sem, w_sem, psend_sem, precv_sem, hsend_sem, hrecv_sem,
):
    me = lax.axis_index("gx")
    head_dim = k_hbm.shape[2]
    ctx = k_hbm.shape[1]
    half = head_dim // 2
    slots = kv_heads * row_count
    groups = part_ref.shape[1] // head_dim - 2
    depth = w_hbm.shape[0]

    k_len = ctx // KEY_CHUNKS
    w_len = depth // WEIGHT_CHUNKS

    local_d = hidden_ref.shape[1]
    d_len = min(head_dim, local_d)
    p_chunks = local_d // d_len

    def proj_copy(c):
        rows = pl.ds(c * d_len, d_len)
        return pltpu.make_async_copy(p_hbm.at[rows], p_vmem.at[rows], p_sem.at[c])

    def key_copy(c):
        rows = pl.ds(c * k_len, k_len)
        return pltpu.make_async_copy(k_hbm.at[0, rows, :], k_vmem.at[rows, :], k_sem.at[c])

    def value_copy(c):
        rows = pl.ds(c * k_len, k_len)
        return pltpu.make_async_copy(v_hbm.at[0, rows, :], v_vmem.at[rows, :], v_sem.at[c])

    def weight_copy(c):
        rows = pl.ds(c * w_len, w_len)
        return pltpu.make_async_copy(w_hbm.at[rows, :], w_vmem.at[rows, :], w_sem.at[c])

    for c in range(p_chunks):
        proj_copy(c).start()

    barrier = pltpu.get_barrier_semaphore()

    @pl.loop(1, n)
    def _(i):
        pl.semaphore_signal(
            barrier, inc=1, device_id={"gx": lax.rem(me + i, n)}, device_id_type=MESH
        )

    for c in range(KEY_CHUNKS):
        key_copy(c).start()
    for c in range(KEY_CHUNKS):
        value_copy(c).start()
    for c in range(WEIGHT_CHUNKS):
        weight_copy(c).start()

    x = hidden_ref[...].astype(jnp.float32)
    scaled = x * gain_ref[...].astype(jnp.float32)
    high = scaled.astype(jnp.bfloat16)
    low = (scaled - high.astype(jnp.float32)).astype(jnp.bfloat16)
    span = d_len * kv_heads
    spread = (
        lax.broadcasted_iota(jnp.int32, (d_len, span), 1) // kv_heads
        == lax.broadcasted_iota(jnp.int32, (d_len, span), 0)
    ).astype(jnp.float32).astype(jnp.bfloat16)
    own_head = (
        lax.broadcasted_iota(jnp.int32, (slots, span), 1) % kv_heads
        == lax.broadcasted_iota(jnp.int32, (slots, span), 0) // row_count
    )
    for c in range(p_chunks):
        for half_index, piece in enumerate((high, low)):
            piece = piece[:, c * d_len:(c + 1) * d_len]
            wide_piece = jnp.dot(piece, spread, preferred_element_type=jnp.float32)
            wide_piece = jnp.concatenate([wide_piece] * kv_heads, axis=0)
            lhs_ref[c, half_index * slots:(half_index + 1) * slots, :] = jnp.where(
                own_head, wide_piece, 0.0
            ).astype(jnp.bfloat16)
    columns = p_hbm.shape[2]
    for c in range(p_chunks):
        proj_copy(c).wait()
        lhs = lhs_ref[c]
        for t in range(0, columns, 256):
            tile = p_vmem[c * d_len:(c + 1) * d_len, :, t:t + 256].reshape(span, 256)
            both = jnp.dot(lhs, tile, preferred_element_type=jnp.float32)
            both = both[:slots] + both[slots:]
            if c == 0:
                part_ref[:, t:t + 256] = both
            else:
                part_ref[:, t:t + 256] += both

    squares = jnp.sum(x * x, axis=1, keepdims=True)
    squares = jnp.concatenate([squares] * kv_heads, axis=0)
    squares = jnp.broadcast_to(squares, (slots, head_dim))
    sq_high = squares.astype(jnp.bfloat16).astype(jnp.float32)
    for g in range(groups + 2):
        wide[:, g, :] = part_ref[:, g * head_dim:(g + 1) * head_dim]
    wide[:, groups + 2, :] = sq_high
    wide[:, groups + 3, :] = squares - sq_high
    for g in range(groups + 4, MSG_ROWS):
        wide[:, g, :] = jnp.zeros((slots, head_dim), jnp.float32)
    send_buf[...] = wide[...].astype(jnp.bfloat16)

    pl.semaphore_wait(barrier, n - 1)

    def part_copy(i):
        peer = lax.rem(me + i, n)
        return pltpu.make_async_remote_copy(
            src_ref=send_buf.at[peer],
            dst_ref=recv_buf.at[i],
            send_sem=psend_sem.at[i],
            recv_sem=precv_sem.at[i],
            device_id={"gx": peer},
            device_id_type=MESH,
        )

    @pl.loop(1, n)
    def _(i):
        part_copy(i).start()

    recv_buf[0] = send_buf[me]

    row = lax.rem(me, row_count)
    place = positions_ref[row].astype(jnp.float32)
    limit = lengths_ref[row]
    angles = freq_ref[...] * place
    cosine = jnp.cos(angles)
    sine = jnp.sin(angles)
    lane = lax.broadcasted_iota(jnp.int32, (1, head_dim), 1)
    sine = jnp.where(lane < half, -sine, sine)

    @pl.loop(1, n)
    def _(i):
        part_copy(i).wait_recv()

    total = jnp.sum(recv_buf[...].astype(jnp.float32), axis=0)
    square_sum = total[groups + 2:groups + 3, :] + total[groups + 3:groups + 4, :]
    projected = total * lax.rsqrt(square_sum / features_total + norm_eps)
    turned = (projected * cosine + pltpu.roll(projected, half, 1) * sine).astype(jnp.bfloat16)
    queries = turned[:groups, :]
    own_key = turned[groups:groups + 1, :]
    own_value = projected[groups + 1:groups + 2, :].astype(jnp.bfloat16)
    entry_ref[...] = jnp.concatenate([own_key, own_value], axis=1)

    scale = head_dim ** (-0.5)
    own_score = (
        jnp.sum(
            queries.astype(jnp.float32) * own_key.astype(jnp.float32), axis=1, keepdims=True
        )
        * scale
    )
    highest = own_score
    for c in range(KEY_CHUNKS):
        key_copy(c).wait()
        s = lax.dot_general(
            queries, k_vmem[c * k_len:(c + 1) * k_len, :], (((1,), (1,)), ((), ())),
            preferred_element_type=jnp.float32,
        ) * scale
        token = c * k_len + lax.broadcasted_iota(jnp.int32, (1, k_len), 1)
        s = jnp.where(token < limit, s, -1e30)
        score_buf[:, c * k_len:(c + 1) * k_len] = s
        highest = jnp.maximum(highest, jnp.max(s, axis=1, keepdims=True))
    own_weight = jnp.exp(own_score - highest)
    denominator = own_weight
    combined = own_weight * own_value.astype(jnp.float32)
    for c in range(KEY_CHUNKS):
        value_copy(c).wait()
        p = jnp.exp(score_buf[:, c * k_len:(c + 1) * k_len] - highest)
        denominator = denominator + jnp.sum(p, axis=1, keepdims=True)
        combined = combined + jnp.dot(
            p.astype(jnp.bfloat16), v_vmem[c * k_len:(c + 1) * k_len, :],
            preferred_element_type=jnp.float32,
        )
    heads_own[...] = (combined / denominator).astype(jnp.bfloat16)

    def heads_copy(i):
        peer = lax.rem(me + i, n)
        return pltpu.make_async_remote_copy(
            src_ref=heads_own,
            dst_ref=heads_all.at[me],
            send_sem=hsend_sem.at[i],
            recv_sem=hrecv_sem.at[me],
            device_id={"gx": peer},
            device_id_type=MESH,
        )

    @pl.loop(1, n)
    def _(i):
        heads_copy(i).start()

    heads_all[me] = heads_own[...]

    for c in range(WEIGHT_CHUNKS):
        weight_copy(c).wait()

    @pl.loop(1, n)
    def _(i):
        source = lax.rem(me + i, n)
        pltpu.make_async_remote_copy(
            src_ref=heads_own,
            dst_ref=heads_all.at[source],
            send_sem=hsend_sem.at[i],
            recv_sem=hrecv_sem.at[source],
            device_id={"gx": source},
            device_id_type=MESH,
        ).wait_recv()

    acc = jnp.zeros(out_ref.shape, jnp.float32)
    width = groups * head_dim
    for h in range(kv_heads):
        block = heads_all[h * row_count:(h + 1) * row_count].astype(jnp.float32)
        for g in range(groups):
            lhs_buf[:, g * head_dim:(g + 1) * head_dim] = block[:, g, :]
        acc = acc + jnp.dot(
            lhs_buf[...].astype(jnp.bfloat16), w_vmem[h * width:(h + 1) * width, :],
            preferred_element_type=jnp.float32,
        )
    out_ref[...] = acc.astype(jnp.bfloat16)

    @pl.loop(1, n)
    def _(i):
        part_copy(i).wait_send()
        heads_copy(i).wait_send()


def local(n, hidden_in, norm_gain, qkv_weight, out_weight, key_cache, value_cache, lengths, positions):
    row_count, local_features = hidden_in.shape
    kv_heads, columns = qkv_weight.shape[1:]
    slot_count, ctx, head_dim = key_cache.shape
    slots = kv_heads * row_count
    assert slot_count == 1 and slots == n
    groups = columns // head_dim - 2
    width = groups * head_dim
    d_len = min(head_dim, local_features)
    p_chunks = local_features // d_len
    index = np.arange(head_dim) % (head_dim // 2)
    freq = jnp.asarray((rope_base ** (-(index * 2.0 / head_dim)))[None, :], jnp.float32)
    vmem = pl.BlockSpec(memory_space=pltpu.VMEM)
    smem = pl.BlockSpec(memory_space=pltpu.SMEM)
    hbm = pl.BlockSpec(memory_space=pl.ANY)
    depth, out_columns = out_weight.shape
    dma = pltpu.SemaphoreType.DMA
    return pl.pallas_call(
        functools.partial(attention_kernel, n, kv_heads, row_count, local_features * n),
        out_shape=(
            jax.ShapeDtypeStruct((row_count, out_columns), jnp.bfloat16),
            jax.ShapeDtypeStruct((1, 2 * head_dim), jnp.bfloat16),
        ),
        in_specs=[smem, smem, vmem, vmem, vmem, hbm, hbm, hbm, hbm],
        out_specs=(vmem, vmem),
        scratch_shapes=[
            pltpu.VMEM(qkv_weight.shape, jnp.bfloat16),
            pltpu.VMEM((p_chunks, 2 * slots, d_len * kv_heads), jnp.bfloat16),
            pltpu.VMEM((slots, columns), jnp.float32),
            pltpu.VMEM((ctx, head_dim), jnp.bfloat16),
            pltpu.VMEM((ctx, head_dim), jnp.bfloat16),
            pltpu.VMEM((depth, out_columns), jnp.bfloat16),
            pltpu.VMEM((slots, MSG_ROWS, head_dim), jnp.float32),
            pltpu.VMEM((slots, MSG_ROWS, head_dim), jnp.bfloat16),
            pltpu.VMEM((n, MSG_ROWS, head_dim), jnp.bfloat16),
            pltpu.VMEM((groups, head_dim), jnp.bfloat16),
            pltpu.VMEM((n, groups, head_dim), jnp.bfloat16),
            pltpu.VMEM((groups, ctx), jnp.float32),
            pltpu.VMEM((row_count, width), jnp.float32),
            dma((p_chunks,)),
            dma((KEY_CHUNKS,)),
            dma((KEY_CHUNKS,)),
            dma((WEIGHT_CHUNKS,)),
            dma((n,)),
            dma((n,)),
            dma((n,)),
            dma((n,)),
        ],
        compiler_params=pltpu.CompilerParams(
            collective_id=0, has_side_effects=True, vmem_limit_bytes=60 * 1024 * 1024
        ),
    )(lengths, positions, freq, hidden_in, norm_gain[None, :], qkv_weight, key_cache, value_cache, out_weight)


def solution(mesh):
    in_specs = (
        P("grp", "gx"),
        P("gx"),
        P("gx", None, None),
        P(None, "gx"),
        P(("grp", "gx"), None, None),
        P(("grp", "gx"), None, None),
        P("grp"),
        P("grp"),
    )
    out_specs = (P("grp", "gx"), P(("grp", "gx"), None))
    return jax.shard_map(
        functools.partial(local, mesh.shape["gx"]),
        mesh=mesh, in_specs=in_specs, out_specs=out_specs, check_vma=False,
    )
```
